1024 devices in a mesh: blk: 16 (over z, x_lo), grp: 64 (over x_hi, y, core).
Axes of the slice: x: 8 (x_hi: 4, x_lo: 2; x = x_hi * 2 + x_lo), y: 8, z: 8, core: 2. Of those that a mesh axis runs over, the one named last changes fastest.
Arguments:
- hamiltonian: bfloat16 [16, 64, 128, 3, 16, 128], P('blk', 'grp'), may hold values from -0.0390625 to 0.0390625
- block_pattern: int32 [16, 64, 3, 16], P('blk', 'grp'), may hold values 0 or 1
- basis_count: int32 [16, 64], P('blk', 'grp'), may hold values from 64 to 128
- probes: bfloat16 [16, 64, 128, 256], P('blk', 'grp'), may hold values from -6 to 6
- coefficients: float32 [5], replicated, may hold values from 0.2 to 1
Outputs:
- fermi_probes: float32 [16, 64, 128, 256], P('blk', 'grp')
The draws below stay inside these ranges and needn't reach their ends.
All inputs are finite; a program needn't handle non-finite values. No bound on the sum of `block_pattern` on one device may be relied on, other than what follows from the above.
Results may differ from the reference program's by a relative error of at most 0.002.
Values may be sent and summed in bfloat16 or wider, within the bound.
A program may use at most 32 MiB of HBM per device.

```python
import jax
import jax.numpy as jnp
from jax import lax

CB = 128
PROBES = 256
KTERMS = 4
N_BLK = 16
N_GRP = 64


def plant(values, key, least, top_value):
    longest = values.shape.index(max(values.shape))
    spots = []
    for shift in (0, 1):
        where = [jax.random.randint(jax.random.fold_in(key, axis), (), 0, length) for axis, length in enumerate(values.shape)]
        where[longest] = (where[longest] + shift) % values.shape[longest]
        spots.append(tuple(where))
    return values.at[spots[0]].set(least).at[spots[1]].set(top_value)


def block_levels(own_key, dims, split, smallest, largest):
    gain = 1.0
    for dim, shards_of in split:
        steps = jax.random.uniform(jax.random.fold_in(jax.random.fold_in(own_key, 6), dim), (shards_of,), jnp.float32, smallest / len(split), largest / len(split))
        gain = gain * jnp.repeat(jnp.exp(steps), dims[dim] // shards_of).reshape((-1,) + (1,) * (len(dims) - 1 - dim))
    return gain


def normal_values(own_key, dims, spread, limit, shards=(), kind=jnp.bfloat16):
    entries = jax.random.normal(own_key, dims, jnp.float32) * spread
    if len(shards) > 0:
        entries = block_levels(own_key, dims, shards, -0.22, 0.18) * entries
    return jnp.clip(entries, min=-limit, max=limit).astype(kind)


def setup_inputs(seed: int = 0) -> dict:
    streams_of = jax.random.split(jax.random.key(seed), 6)
    return {
        "hamiltonian": normal_values(streams_of[0], (N_BLK, N_GRP, CB, 3, N_BLK, CB), (12 * N_BLK * CB) ** -0.5, 0.0390625, ((0, 16), (1, 64))),
        "block_pattern": plant((jax.random.randint(streams_of[1], (N_BLK, N_GRP, 3, N_BLK), 0, 4) < 3).astype(jnp.int32), jax.random.fold_in(streams_of[1], 1), 0, 1),
        "basis_count": plant(jax.random.randint(streams_of[2], (N_BLK, N_GRP), CB // 2, CB + 1), jax.random.fold_in(streams_of[2], 1), CB // 2, CB).astype(jnp.int32),
        "probes": normal_values(streams_of[3], (N_BLK, N_GRP, CB, PROBES), 1.0, 6.0, ((0, 16), (1, 64))),
        "coefficients": jnp.clip(jax.random.uniform(streams_of[4], (KTERMS + 1,), jnp.float32, 0.2, 1.0), 0.2, 1.0),
    }


def apply_once(term, hamiltonian, block_pattern, live):
    stacked = jnp.stack([jnp.roll(term, 1, axis=1), term, jnp.roll(term, -1, axis=1)], 0).astype(jnp.float32)

    def one_block(pair):
        rows, pattern = pair
        kept = rows.astype(jnp.float32) * pattern[:, None, :, :, None].astype(jnp.float32)
        return jnp.einsum('gidjc,djgcp->gip', kept, stacked)

    result = lax.map(one_block, (hamiltonian, block_pattern))
    return result * live


def reference(hamiltonian, block_pattern, basis_count, probes, coefficients):
    live = (jnp.arange(CB)[None, None, :] < basis_count[:, :, None]).astype(jnp.float32)[..., None]
    first = (probes.astype(jnp.float32) * live).astype(jnp.bfloat16)
    older = first.astype(jnp.float32)
    newer = apply_once(first, hamiltonian, block_pattern, live)
    total = coefficients[0] * older + coefficients[1] * newer
    for order in range(2, KTERMS + 1):
        nextterm = 2.0 * apply_once(newer.astype(jnp.bfloat16), hamiltonian, block_pattern, live) - older
        older, newer = newer, nextterm
        total = total + coefficients[order] * newer
    return total
```

```python
import functools

import jax
import jax.numpy as jnp
from jax import lax
from jax.experimental import pallas as pl
from jax.experimental.pallas import tpu as pltpu
from jax.sharding import PartitionSpec as P

MESH = pl.DeviceIdType.MESH
TERMS = 4

CHUNKS = 2
LAG = 0


def kernel(
    n_z, n_grp,
    pattern, count, coefficients, hamiltonian, probes, out,
    raw, wide, rows, lent, held, part, arrived, term, own,
    raw_sem, lent_sem, rows_sem, sent_sem, own_sem, pair_sem, low_sem, part_sem,
):
    blk, grp = lax.axis_index("blk"), lax.axis_index("grp")
    z, x = blk // 2, blk % 2
    slots, width = held.shape[3], held.shape[4]
    half = slots // 2

    def place(dz):
        return lax.rem(z + n_z + dz, n_z)

    ahead = {1: (place(1) * 2 + x, grp), -1: (place(-1) * 2 + x, grp)}
    partner = (z * 2 + 1 - x, grp)
    after = (blk, lax.rem(grp + 1, n_grp))
    before = (blk, lax.rem(grp + n_grp - 1, n_grp))

    def send(source, target, sem_out, sem_in, device):
        pltpu.make_async_remote_copy(
            src_ref=source, dst_ref=target, send_sem=sem_out, recv_sem=sem_in,
            device_id=device, device_id_type=MESH,
        ).start()

    def landed(ref, sem):
        pltpu.make_async_copy(ref, ref, sem).wait()

    for d in (2, 0, 1):
        pltpu.make_async_copy(hamiltonian.at[:, d], raw.at[d], raw_sem.at[d]).start()

    barrier = pltpu.get_barrier_semaphore()
    for device in (ahead[1], ahead[-1], partner, after, before):
        pl.semaphore_signal(barrier, inc=1, device_id=device, device_id_type=MESH)

    live = lax.broadcasted_iota(jnp.int32, (slots, width), 0) < count[0, 0]

    for q in range(CHUNKS):
        lanes = slice(q * width, (q + 1) * width)
        first = jnp.where(live, probes[:, lanes].astype(jnp.float32), 0.0)
        term[0, q] = first
        out[:, lanes] = coefficients[0] * first
        held[0, q, blk] = first.astype(jnp.bfloat16)

    def regroup(d, target, at):
        landed(raw.at[d], raw_sem.at[d])
        wide[...] = raw[d].astype(jnp.float32).reshape(wide.shape)
        for c in range(2 * n_z):
            block = wide[pl.ds(c, slots, stride=2 * n_z), :] * pattern[d, c].astype(jnp.float32)
            target[c // 2, at:at + slots, (c % 2) * slots:(c % 2 + 1) * slots] = block.astype(jnp.bfloat16)

    def chunk(q):
        reach = {1: 4, -1: 3} if q % 2 == 0 else {1: 3, -1: 4}
        lanes = slice(q * width, (q + 1) * width)
        for k in range(TERMS):
            v = held.at[k, q]
            out_sem = sent_sem.at[k, q]

            def own_ref(s, h):
                return v.at[place(-s * h) * 2 + x]

            def pair_ref(s, h):
                return v.at[place(-s * h) * 2 + 1 - x, 0:half]

            def low_ref(s, h, side):
                return v.at[place(-s * h) * 2 + side, half:slots]

            def own_on(s, h):
                send(own_ref(s, h), own_ref(s, h), out_sem, own_sem.at[k, q, (s + 1) // 2, h], ahead[s])

            def pair_on(s, h):
                send(pair_ref(s, h), pair_ref(s, h), out_sem, pair_sem.at[k, q, (s + 1) // 2, h], ahead[s])

            own_on(1, 0)
            own_on(-1, 0)
            send(v.at[blk], v.at[blk], out_sem, low_sem.at[k, q, 0, 0], partner)
            yield
            for h in range(1, 5):
                if h == 1:
                    landed(v.at[z * 2 + 1 - x], low_sem.at[k, q, 0, 0])
                    pair_on(1, 0)
                    pair_on(-1, 0)
                for s in (1, -1):
                    if h <= reach[s]:
                        landed(own_ref(s, h), own_sem.at[k, q, (s + 1) // 2, h - 1])
                        if h < reach[s]:
                            own_on(s, h)
                        send(low_ref(s, h, x), low_ref(s, h, x), out_sem, low_sem.at[k, q, (s + 1) // 2, h], partner)
                if h > 1:
                    for s in (1, -1):
                        if h - 1 <= reach[-s]:
                            landed(pair_ref(s, h - 1), pair_sem.at[k, q, (s + 1) // 2, h - 2])
                            if h - 1 < reach[-s]:
                                pair_on(s, h - 1)
                yield
            for s in (1, -1):
                if 4 <= reach[-s]:
                    landed(pair_ref(s, 4), pair_sem.at[k, q, (s + 1) // 2, 3])
            for h in range(1, 5):
                for s in (1, -1):
                    if h <= reach[s]:
                        landed(low_ref(s, h, 1 - x), low_sem.at[k, q, (s + 1) // 2, h])
            if k == 0 and q == 0:
                landed(rows.at[:, 0:slots], rows_sem.at[0])
                landed(rows.at[:, 2 * slots:3 * slots], rows_sem.at[1])
            product = jnp.zeros((3 * slots, width), jnp.float32)
            for c in range(n_z):
                product += jnp.dot(
                    rows[c], v[2 * c:2 * c + 2].reshape(2 * slots, width), preferred_element_type=jnp.float32
                )
            part[k, q, 0] = product[0:slots]
            part[k, q, 1] = product[2 * slots:3 * slots]
            send(part.at[k, q, 0], arrived.at[k, q, 1], out_sem, part_sem.at[k, q, 1], before)
            send(part.at[k, q, 1], arrived.at[k, q, 0], out_sem, part_sem.at[k, q, 0], after)
            own[q] = product[slots:2 * slots]
            yield
            for side in range(2):
                landed(arrived.at[k, q, side], part_sem.at[k, q, side])
            applied = jnp.where(live, own[q] + arrived[k, q, 0] + arrived[k, q, 1], 0.0)
            new = applied if k == 0 else 2.0 * applied - term[(k + 1) % 2, q]
            if k + 1 < TERMS:
                held[k + 1, q, blk] = new.astype(jnp.bfloat16)
                term[(k + 1) % 2, q] = new
            out[:, lanes] = out[:, lanes] + coefficients[k + 1] * new

    regroup(2, lent.at[0], 0)
    regroup(0, lent.at[1], 0)
    pl.semaphore_wait(barrier, 5)

    chunks = [chunk(q) for q in range(CHUNKS)]
    next(chunks[0])
    send(lent.at[0], rows.at[:, 0:slots], lent_sem.at[0], rows_sem.at[0], after)
    send(lent.at[1], rows.at[:, 2 * slots:3 * slots], lent_sem.at[1], rows_sem.at[1], before)
    regroup(1, rows, slots)
    turn = 1
    running = list(range(CHUNKS))
    while running:
        for q in list(running):
            if turn < q * LAG:
                continue
            try:
                next(chunks[q])
            except StopIteration:
                running.remove(q)
        turn += 1

    for i in range(2):
        landed(lent.at[i], lent_sem.at[i])
    for k in range(TERMS):
        for q in range(CHUNKS):
            landed(held.at[k, q, 0:2 * n_z - 1], sent_sem.at[k, q])
            landed(part.at[k, q], sent_sem.at[k, q])


def local(hamiltonian, block_pattern, basis_count, probes, coefficients):
    slots, near, blocks, _ = hamiltonian.shape[2:]
    count = probes.shape[3]
    width = count // CHUNKS
    n_z = blocks // 2
    vmem, smem = pl.BlockSpec(memory_space=pltpu.VMEM), pl.BlockSpec(memory_space=pltpu.SMEM)
    dma = pltpu.SemaphoreType.DMA
    result = pl.pallas_call(
        functools.partial(kernel, n_z, lax.axis_size("grp")),
        out_shape=jax.ShapeDtypeStruct((slots, count), jnp.float32),
        in_specs=[smem, smem, smem, pl.BlockSpec(memory_space=pl.ANY), vmem],
        out_specs=vmem,
        scratch_shapes=[
            pltpu.VMEM((near, slots, blocks, slots), jnp.bfloat16),
            pltpu.VMEM((slots * blocks, slots), jnp.float32),
            pltpu.VMEM((n_z, near * slots, 2 * slots), jnp.bfloat16),
            pltpu.VMEM((2, n_z, slots, 2 * slots), jnp.bfloat16),
            pltpu.VMEM((TERMS, CHUNKS, blocks, slots, width), jnp.bfloat16),
            pltpu.VMEM((TERMS, CHUNKS, 2, slots, width), jnp.float32),
            pltpu.VMEM((TERMS, CHUNKS, 2, slots, width), jnp.float32),
            pltpu.VMEM((2, CHUNKS, slots, width), jnp.float32),
            pltpu.VMEM((CHUNKS, slots, width), jnp.float32),
            dma((near,)),
            dma((2,)),
            dma((2,)),
            dma((TERMS, CHUNKS)),
            dma((TERMS, CHUNKS, 2, 4)),
            dma((TERMS, CHUNKS, 2, 4)),
            dma((TERMS, CHUNKS, 2, 5)),
            dma((TERMS, CHUNKS, 2)),
        ],
        compiler_params=pltpu.CompilerParams(
            collective_id=0, has_side_effects=True, vmem_limit_bytes=32 * 1024 * 1024
        ),
        cost_estimate=pl.CostEstimate(
            flops=2 * TERMS * near * slots * blocks * slots * count, bytes_accessed=2 * hamiltonian.size, transcendentals=0
        ),
    )(block_pattern[0, 0], basis_count, coefficients, hamiltonian[0, 0], probes[0, 0])
    return result[None, None]


def solution(mesh):
    placed = (
        P("blk", "grp", None, None, None, None),
        P("blk", "grp", None, None),
        P("blk", "grp"),
        P("blk", "grp", None, None),
        P(),
    )
    return jax.shard_map(
        local, mesh=mesh, in_specs=placed, out_specs=P("blk", "grp", None, None), check_vma=False
    )
```

```python
import functools

import jax
import jax.numpy as jnp
from jax import lax
from jax.experimental import pallas as pl
from jax.experimental.pallas import tpu as pltpu
from jax.sharding import PartitionSpec as P

MESH = pl.DeviceIdType.MESH
TERMS = 4

SUB = 4
TOP = 0
PLAN = {1: 0, -1: 0, 2: 1, -2: -1, 3: 2, -3: -2, 4: 3}
WAITS = [(0, 1), (0, -1), (1, 0), (0, 2), (0, -2), (1, 1), (1, -1), (0, 3), (0, -3), (1, 2), (1, -2), (0, 4), (1, 3), (1, -3), (1, 4)]
EARLY = 5
FAR, NEAR, OWN = 0, 1, 2

ORDER = (0, *PLAN)
HOPS = sorted({abs(to - by) for to, by in PLAN.items()})


def kernel(
    n_z, n_grp,
    pattern_in, count_in, coefficients_in, hamiltonian, probes_in, out,
    pattern, count, coefficients, probes,
    raw, wide, rows, lent, held, part, arrived, term, sums,
    in_sem, raw_sem, lent_sem, rows_sem, sent_sem, line_sem, cross_sem, part_sem,
):
    blk, grp = lax.axis_index("blk"), lax.axis_index("grp")
    z, x, core = blk // 2, blk % 2, grp % 2
    slots, width = probes.shape
    piece = slots // SUB

    inputs = [
        pltpu.make_async_copy(source, target, in_sem.at[i])
        for i, (source, target) in enumerate((
            (probes_in.at[0, 0], probes), (count_in, count), (coefficients_in, coefficients),
            (pattern_in.at[0, 0], pattern),
        ))
    ]
    for copy in inputs:
        copy.start()
    third = {FAR: 2 * core, NEAR: 2 - 2 * core, OWN: 1}
    for side in (FAR, NEAR, OWN):
        pltpu.make_async_copy(hamiltonian.at[0, 0, :, third[side]], raw.at[side], raw_sem.at[side]).start()

    def along(dz):
        return (lax.rem(z + n_z + dz, n_z) * 2 + x, grp)

    partner = (z * 2 + 1 - x, grp)
    beside = {
        FAR: (blk, lax.rem(grp + n_grp + 2 * core - 1, n_grp)),
        NEAR: (blk, grp + 1 - 2 * core),
    }

    barrier = pltpu.get_barrier_semaphore()
    peers = [along(h) for h in HOPS] + [along(-h) for h in HOPS if 2 * h != n_z] + [partner, *beside.values()]
    for device in peers:
        pl.semaphore_signal(barrier, inc=1, device_id=device, device_id_type=MESH)

    def send(source, target, sem_out, sem_in, device):
        pltpu.make_async_remote_copy(
            src_ref=source, dst_ref=target, send_sem=sem_out, recv_sem=sem_in,
            device_id=device, device_id_type=MESH,
        ).start()

    def landed(ref, sem):
        pltpu.make_async_copy(ref, ref, sem).wait()

    def lies(j, across, p):
        return pl.ds((ORDER.index(j) * 2 + across) * slots + p * piece, piece)

    def forward(k, j, across, p):
        sems = cross_sem if across else line_sem
        for to, by in PLAN.items():
            if by == j:
                send(
                    held.at[k, lies(j, across, p)], held.at[k, lies(to, across, p)],
                    sent_sem.at[k], sems.at[k, ORDER.index(to), p], along(to - j),
                )
        if not across and (j == 0 or p >= TOP):
            send(
                held.at[k, lies(j, 0, p)], held.at[k, lies(j, 1, p)],
                sent_sem.at[k], cross_sem.at[k, ORDER.index(j), p], partner,
            )

    def regroup(side, target):
        landed(raw.at[side], raw_sem.at[side])
        wide[...] = raw[side].astype(jnp.float32).reshape(wide.shape)
        for c in range(2 * n_z):
            block = wide[pl.ds(c, slots, stride=2 * n_z), :] * pattern[third[side], c].astype(jnp.float32)
            offset = lax.rem(z + n_z - c // 2, n_z)
            at = 0
            for n, j in enumerate(ORDER):
                at += jnp.where(offset == j % n_z, n, 0)
            at = at * 2 + jnp.where(x == c % 2, 0, 1)
            target[:, pl.ds(pl.multiple_of(at * slots, slots), slots)] = block.astype(jnp.bfloat16)

    for copy in inputs:
        copy.wait()
    live = lax.broadcasted_iota(jnp.int32, (slots, width), 0) < count[0, 0]
    first = jnp.where(live, probes[...].astype(jnp.float32), 0.0)
    held[0, 0:slots] = first.astype(jnp.bfloat16)
    pl.semaphore_wait(barrier, len(peers))
    for p in range(SUB):
        forward(0, 0, 0, p)
    term[0] = first
    out[...] = coefficients[0] * first
    for side in (FAR, NEAR):
        regroup(side, lent.at[side])
        send(lent.at[side], rows.at[side], lent_sem.at[side], rows_sem.at[side], beside[side])
    regroup(OWN, rows.at[OWN])

    def add(k, side, low, high, fresh):
        product = jnp.dot(
            rows[side, :, 2 * low * slots:2 * high * slots], held[k, 2 * low * slots:2 * high * slots],
            preferred_element_type=jnp.float32,
        )
        return product if fresh else sums[side] + product

    for k in range(TERMS):
        def arrive(across, j):
            for p in range(TOP if across else SUB):
                landed(held.at[k, lies(j, across, p)], (cross_sem if across else line_sem).at[k, ORDER.index(j), p])
                forward(k, j, across, p)

        def crossed(j):
            for p in range(TOP, SUB):
                landed(held.at[k, lies(j, 1, p)], cross_sem.at[k, ORDER.index(j), p])

        for across, j in WAITS:
            arrive(across, j)
        for j in ORDER[0:EARLY]:
            crossed(j)
        if k == 0:
            for side in (FAR, NEAR):
                landed(rows.at[side], rows_sem.at[side])
        if EARLY < n_z:
            for side in (FAR, NEAR, OWN):
                sums[side] = add(k, side, 0, EARLY, True)
        for j in ORDER[EARLY:]:
            crossed(j)
        late = (0, n_z, True) if EARLY == n_z else (EARLY, n_z, False)
        for side in (FAR, NEAR):
            part[k, side] = add(k, side, *late)
            for p in range(SUB):
                some = pl.ds(p * piece, piece)
                send(
                    part.at[k, side, some], arrived.at[k, side, some],
                    sent_sem.at[k], part_sem.at[k, side, p], beside[side],
                )
        sums[OWN] = add(k, OWN, *late)
        if k > 0:
            out[...] = out[...] + coefficients[k] * term[k % 2]
        for p in range(SUB):
            piece_rows = slice(p * piece, (p + 1) * piece)
            for side in (NEAR, FAR):
                landed(arrived.at[k, side, piece_rows], part_sem.at[k, side, p])
            alive = lax.broadcasted_iota(jnp.int32, (piece, width), 0) + p * piece < count[0, 0]
            new = sums[OWN, piece_rows] + arrived[k, NEAR, piece_rows] + arrived[k, FAR, piece_rows]
            new = jnp.where(alive, new, 0.0)
            if k > 0:
                new = 2.0 * new - term[(k + 1) % 2, piece_rows]
            if k + 1 < TERMS:
                held[k + 1, piece_rows] = new.astype(jnp.bfloat16)
                forward(k + 1, 0, 0, p)
                term[(k + 1) % 2, piece_rows] = new
            else:
                out[piece_rows] = out[piece_rows] + coefficients[TERMS] * new

    for side in (FAR, NEAR):
        landed(lent.at[side], lent_sem.at[side])
    for k in range(TERMS):
        landed(held.at[k, 0:(2 * n_z - 1) * slots], sent_sem.at[k])
        landed(part.at[k], sent_sem.at[k])


def local(hamiltonian, block_pattern, basis_count, probes, coefficients):
    slots, near, blocks, _ = hamiltonian.shape[2:]
    width = probes.shape[3]
    n_z = blocks // 2
    dma = pltpu.SemaphoreType.DMA
    hbm = pl.BlockSpec(memory_space=pl.ANY)
    result = pl.pallas_call(
        functools.partial(kernel, n_z, lax.axis_size("grp")),
        out_shape=jax.ShapeDtypeStruct((slots, width), jnp.float32),
        in_specs=[hbm] * 5,
        out_specs=pl.BlockSpec(memory_space=pltpu.VMEM),
        scratch_shapes=[
            pltpu.SMEM(block_pattern.shape[2:], jnp.int32),
            pltpu.SMEM(basis_count.shape, jnp.int32),
            pltpu.SMEM(coefficients.shape, jnp.float32),
            pltpu.VMEM((slots, width), jnp.bfloat16),
            pltpu.VMEM((near, slots, blocks, slots), jnp.bfloat16),
            pltpu.VMEM((slots * blocks, slots), jnp.float32),
            pltpu.VMEM((near, slots, blocks * slots), jnp.bfloat16),
            pltpu.VMEM((2, slots, blocks * slots), jnp.bfloat16),
            pltpu.VMEM((TERMS, blocks * slots, width), jnp.bfloat16),
            pltpu.VMEM((TERMS, 2, slots, width), jnp.float32),
            pltpu.VMEM((TERMS, 2, slots, width), jnp.float32),
            pltpu.VMEM((2, slots, width), jnp.float32),
            pltpu.VMEM((near, slots, width), jnp.float32),
            dma((4,)),
            dma((near,)),
            dma((2,)),
            dma((2,)),
            dma((TERMS,)),
            dma((TERMS, n_z, SUB)),
            dma((TERMS, n_z, SUB)),
            dma((TERMS, 2, SUB)),
        ],
        compiler_params=pltpu.CompilerParams(
            collective_id=0, has_side_effects=True, vmem_limit_bytes=60 * 1024 * 1024
        ),
        cost_estimate=pl.CostEstimate(
            flops=2 * TERMS * near * slots * blocks * slots * width, bytes_accessed=2 * hamiltonian.size, transcendentals=0
        ),
    )(block_pattern, basis_count, coefficients, hamiltonian, probes)
    return result[None, None]


def solution(mesh):
    placed = (
        P("blk", "grp", None, None, None, None),
        P("blk", "grp", None, None),
        P("blk", "grp"),
        P("blk", "grp", None, None),
        P(),
    )
    return jax.shard_map(
        local, mesh=mesh, in_specs=placed, out_specs=P("blk", "grp", None, None), check_vma=False
    )
```
